256 devices in a mesh: dp: 4 (over z_lo), pipe: 4 (over y), tensor: 16 (over z_hi, x, core).
Axes of the slice: x: 4, y: 4, z: 8 (z_hi: 2, z_lo: 4; z = z_hi * 4 + z_lo), core: 2. Of those that a mesh axis runs over, the one named last changes fastest.
Arguments:
- outgoing: bfloat16 [4, 512, 8192], P('pipe', 'dp', 'tensor'), may hold values from -40 to 40
- stashed_inputs: bfloat16 [4, 512, 8192], P('pipe', 'dp', 'tensor'), may hold values from -1.5 to 1.5
- encoder: bfloat16 [4, 8192, 1024], P('pipe', 'tensor'), may hold values from -0.0625 to 0.0625
- decoder: bfloat16 [4, 1024, 8192], P('pipe', None, ('dp', 'tensor')), may hold values from -0.28125 to 0.28125
- norm_gain: float32 [4, 8192], P('pipe', 'dp'), may hold values from 0.1 to 1.9
- gate_matrix: bfloat16 [4, 8192, 14336], P('pipe', 'dp', 'tensor'), may hold values from -0.0625 to 0.0625
- up_matrix: bfloat16 [4, 8192, 14336], P('pipe', 'dp', 'tensor'), may hold values from -0.0625 to 0.0625
- grad_decoded: bfloat16 [4, 512, 8192], P('pipe', None, ('dp', 'tensor')), may hold values from -1.5 to 1.5
- stashed_codes: bfloat16 [4, 512, 1024], P('pipe', ('dp', 'tensor')), may hold values from -4 to 4
Outputs:
- activated: bfloat16 [4, 512, 14336], P('pipe', 'dp', 'tensor')
- input_grad: bfloat16 [4, 512, 8192], P('pipe', 'dp', 'tensor')
- encoder_grad: float32 [4, 8192, 1024], P('pipe', 'tensor', 'dp')
- decoder_grad: float32 [4, 1024, 8192], P('pipe', None, ('dp', 'tensor'))
The draws below stay inside these ranges and needn't reach their ends.
All inputs are finite; a program needn't handle non-finite values.
Results may differ from the reference program's by a relative error of at most 0.0082.
Values may be sent and summed in bfloat16 or wider, within the bound.
A program may use at most 64 MiB of HBM per device.

```python
import math
import jax
import jax.numpy as jnp
from jax import lax

D = 8192
C = 1024
FF = 14336
SECTIONS = 4
TOKENS = 512


def draw_outgoing(key, part):
    key = jax.random.fold_in(key, 11)
    noise_key, scale_key = jax.random.split(key, 2)
    shape = (SECTIONS, TOKENS, D)
    values = jnp.clip(jax.random.normal(noise_key, shape, jnp.float32), -4.0, 4.0)
    spread = jnp.exp(jax.random.uniform(scale_key, (SECTIONS, TOKENS, 1), jnp.float32) * math.log(10.0))
    return (values * spread).astype(jnp.bfloat16)


def draw_decoder(key, part):
    key = jax.random.fold_in(key, 23)
    noise_key, scale_key = jax.random.split(key, 2)
    shape = (SECTIONS, C, D)
    values = jnp.clip(jax.random.normal(noise_key, shape, jnp.float32), -3.0, 3.0)
    columns = 0.3 * jnp.exp(jax.random.uniform(scale_key, (SECTIONS, 1, D), jnp.float32) * math.log(10.0))
    return (values * columns / 32.0).astype(jnp.bfloat16)


def block_levels(own_key, dims, cuts, smallest, high):
    level = 1.0
    for axis_at, parts in cuts:
        heights = jax.random.uniform(jax.random.fold_in(jax.random.fold_in(own_key, 6), axis_at), (parts,), jnp.float32, smallest / len(cuts), high / len(cuts))
        level = level * jnp.repeat(jnp.exp(heights), dims[axis_at] // parts).reshape((-1,) + (1,) * (len(dims) - 1 - axis_at))
    return level


def scatter_about(key, dims, deviation, bound, cuts=(), dtype=jnp.bfloat16):
    result = deviation * jax.random.normal(key, dims, jnp.float32)
    if cuts:
        result = result * block_levels(key, dims, cuts, -0.22, 0.18)
    return jnp.clip(result, -bound, bound).astype(dtype)


def setup_inputs(seed: int = 0) -> dict:
    seeds = jax.random.split(jax.random.key(seed), 10)
    return {
        "outgoing": draw_outgoing(jax.random.fold_in(seeds[9], 71), 0),
        "stashed_inputs": scatter_about(seeds[1], (SECTIONS, TOKENS, D), 0.25, 1.5, ((0, 4), (1, 4), (2, 16))),
        "encoder": scatter_about(seeds[2], (SECTIONS, D, C), D ** -0.5, 0.0625, ((0, 4), (1, 16))),
        "decoder": draw_decoder(jax.random.fold_in(seeds[9], 71), 0),
        "norm_gain": jnp.clip(1.0 + 0.18 * jax.random.normal(seeds[4], (SECTIONS, D), jnp.float32), 0.1, 1.9),
        "gate_matrix": scatter_about(seeds[5], (SECTIONS, D, FF), D ** -0.5, 0.0625, ((0, 4), (1, 4), (2, 16))),
        "up_matrix": scatter_about(seeds[6], (SECTIONS, D, FF), D ** -0.5, 0.0625, ((0, 4), (1, 4), (2, 16))),
        "grad_decoded": scatter_about(seeds[7], (SECTIONS, TOKENS, D), 0.25, 1.5, ((0, 4), (2, 64))),
        "stashed_codes": scatter_about(seeds[8], (SECTIONS, TOKENS, C), 1.0, 4.0, ((0, 4), (1, 64))),
    }


epsilon = 1e-05

def reference(outgoing, stashed_inputs, encoder, decoder, norm_gain, gate_matrix, up_matrix, grad_decoded, stashed_codes):
    section_count = outgoing.shape[0]
    codes_out = [jnp.dot(outgoing[section], encoder[section], preferred_element_type=jnp.float32).astype(jnp.bfloat16) for section in range(section_count)]
    grads_out = [jnp.dot(grad_decoded[section], decoder[section].T, preferred_element_type=jnp.float32).astype(jnp.bfloat16) for section in range(section_count)]
    zero_code = jnp.zeros_like(codes_out[0])
    activated_list, input_list, encoder_list, decoder_list = ([], [], [], [])
    for section in range(section_count):
        incoming = codes_out[section - 1] if section > 0 else zero_code
        decoded = jnp.dot(incoming, decoder[section], preferred_element_type=jnp.float32).astype(jnp.bfloat16)
        widened = decoded.astype(jnp.float32)
        inv_rms = lax.rsqrt(lax.optimization_barrier(jnp.sum(widened * widened, axis=1, keepdims=True)) / D + epsilon)
        normed = (widened * norm_gain[section][None, :]).astype(jnp.bfloat16)
        gate_val = inv_rms * jnp.dot(normed, gate_matrix[section], preferred_element_type=jnp.float32)
        up_val = inv_rms * jnp.dot(normed, up_matrix[section], preferred_element_type=jnp.float32)
        activated_list.append((jax.nn.silu(gate_val) * up_val).astype(jnp.bfloat16))
        returned = grads_out[section + 1] if section + 1 < section_count else zero_code
        input_list.append(jnp.dot(returned, encoder[section].T, preferred_element_type=jnp.float32).astype(jnp.bfloat16))
        encoder_list.append(jnp.dot(stashed_inputs[section].T, returned, preferred_element_type=jnp.float32))
        decoder_list.append(jnp.dot(stashed_codes[section].T, grad_decoded[section], preferred_element_type=jnp.float32))
    return (jnp.stack(activated_list), jnp.stack(input_list), jnp.stack(encoder_list), jnp.stack(decoder_list))
```

```python
import jax
import jax.numpy as jnp
from jax import lax
from jax.experimental import pallas as pl
from jax.experimental.pallas import tpu as pltpu
from jax.sharding import PartitionSpec as P

D = 8192
epsilon = 1e-05
MESH = pl.DeviceIdType.MESH
F32 = jnp.float32
BF16 = jnp.bfloat16

LAST = (((1,), (1,)), ((), ()))
FIRST = (((0,), (0,)), ((), ()))


def kernel(
    out_h,
    stin_h,
    enc_h,
    dec_h,
    gain_h,
    gate_h,
    up_h,
    grad_h,
    stc_v,
    act_o,
    ing_o,
    encg_o,
    decg_o,
    out_v,
    enc_v,
    gain_v,
    grad_v,
    stin_v,
    wgu,
    w_all,
    q_send,
    q_recv,
    q_own,
    x_recv,
    r_own,
    z_recv,
    code_sh,
    code,
    blk,
    blk_r,
    st_sh,
    st,
    ga,
    pb,
    pb_r,
    cg_sh,
    ret,
    normed,
    acc,
    gu_s,
    gu_r,
    gu_own,
    ssq,
    ssq_r,
    local_sem,
    wload_sem,
    s_core,
    r_core,
    s_x,
    r_x,
    s_z,
    r_z,
    s_gu,
    r_gu,
):
    dp = lax.axis_index("dp")
    y = lax.axis_index("pipe")
    t = lax.axis_index("tensor")
    zh = t // 8
    x = (t // 2) % 4
    c = t % 2
    z = zh * 4 + dp

    def dev(z_, y_, x_, c_):
        return (z_ % 4, y_, (z_ // 4) * 8 + x_ * 2 + c_)

    sib = dev(z, y, x, 1 - c)
    xs = [(x + k) % 4 for k in range(4)]
    xdev = [dev(z, y, v, c) for v in xs]
    zdev = [dev((z + k) % 8, y, x, c) for k in range(8)]
    updev = [dev((z + k) % 8, (y + 1) % 4, x, c) for k in range(8)]
    downdev = [dev((z + k) % 8, (y + 3) % 4, x, c) for k in range(8)]
    far = [dev((z + 4) % 8, y, v, c) for v in xs]
    dpdev = [((dp + k) % 4, y, t) for k in range(4)]

    def half(c_):
        return pl.ds(pl.multiple_of(c_ * 512, 512), 512)

    own_half = half(c)
    own_lane = pl.ds(pl.multiple_of(c * 128, 128), 128)
    slab = pl.ds(pl.multiple_of((dp * 2 + zh) * 16, 16), 16)

    pending = []

    def send(src, dst, ss, rs, to):
        cp = pltpu.make_async_remote_copy(
            src_ref=src, dst_ref=dst, send_sem=ss, recv_sem=rs, device_id=to, device_id_type=MESH
        )
        cp.start()
        pending.append(cp)
        return cp

    def local(src, dst, sem):
        cp = pltpu.make_async_copy(src, dst, sem)
        cp.start()
        return cp

    l_out = local(out_h.at[0], out_v, local_sem.at[0])
    l_enc = local(enc_h.at[0], enc_v, local_sem.at[1])
    own_w = w_all.at[zh * 4 + x, :, own_lane]
    l_dec = local(dec_h.at[0], own_w, local_sem.at[2])
    own_slot = pl.ds(pl.multiple_of((zh * 4 + x) * 128, 128), 128)
    own_rows = pl.ds(pl.multiple_of(x * 32 + zh * 16, 16), 16)
    l_ga = local(grad_h.at[:, own_rows, :], ga.at[c, :, :, own_slot], local_sem.at[3])
    l_grad = local(grad_h, grad_v, local_sem.at[4])
    l_gain = local(gain_h, gain_v, local_sem.at[5])
    l_stin = local(stin_h.at[0], stin_v.at[dp], local_sem.at[6])
    l_gu = []
    for n in range(7):
        cols = pl.ds(n * 128, 128)
        l_gu.append(local(gate_h.at[0, :, cols], wgu.at[n, :, pl.ds(0, 128)], wload_sem.at[2 * n]))
        l_gu.append(local(up_h.at[0, :, cols], wgu.at[n, :, pl.ds(128, 128)], wload_sem.at[2 * n + 1]))

    barrier = pltpu.get_barrier_semaphore()
    peers = [sib] + xdev[1:] + zdev[1:] + updev + downdev + far[1:]
    for p in peers:
        pl.semaphore_signal(barrier, inc=1, device_id=p, device_id_type=MESH)
    pl.semaphore_wait(barrier, len(peers))

    wz = send(dec_h.at[0], own_w, s_z.at[0], r_z.at[0], zdev[4])
    ga_in = []
    for k in range(4):
        for h in range(2):
            if k == 0 and h == 0:
                continue
            zh_to = (zh + h) % 2
            rows = pl.ds(pl.multiple_of(xs[k] * 32 + zh_to * 16, 16), 16)
            to = far[k] if h else xdev[k]
            i = k * 2 + h
            ga_in.append(
                send(grad_h.at[:, rows, :], ga.at[c, :, :, own_slot], s_x.at[i], r_x.at[i], to)
            )

    l_out.wait()
    l_enc.wait()
    q_send[...] = jnp.dot(out_v[...], enc_v[:, half(1 - c)], preferred_element_type=F32)
    qc = send(q_send, q_recv, s_core.at[0], r_core.at[0], sib)
    stc = stc_v[0].astype(F32)
    blk[...] = jnp.concatenate([stc[:, :512], stc[:, 512:]], axis=0).astype(BF16)
    bc = send(blk, blk_r, s_core.at[1], r_core.at[1], sib)
    q_own[...] = jnp.dot(out_v[...], enc_v[:, own_half], preferred_element_type=F32)
    qc.wait_recv()
    q_own[...] += q_recv[...]
    xr = []
    for k in range(1, 4):
        rows = pl.ds(pl.multiple_of(xs[k] * 32, 32), 32)
        xr.append(send(q_own.at[rows, :], x_recv.at[k - 1], s_x.at[7 + k], r_x.at[7 + k], xdev[k]))
    wx = [send(dec_h.at[0], own_w, s_x.at[10 + k], r_x.at[10 + k], xdev[k]) for k in range(1, 4)]
    wc = [send(dec_h.at[0], own_w, s_core.at[2], r_core.at[2], sib)]

    bc.wait_recv()
    a = blk[...].astype(F32)
    b = blk_r[...].astype(F32)
    mine = jnp.where(c == 0, a[:8], a[8:])
    other = jnp.where(c == 0, b[:8], b[8:])
    first = jnp.where(c == 0, mine, other)
    second = jnp.where(c == 0, other, mine)
    st_val = jnp.concatenate([first, second], axis=0).astype(BF16)
    st_sh[...] = st_val
    st[x, slab, own_half] = st_val

    for cp in xr:
        cp.wait_recv()
    r_own[...] = (
        q_own[pl.ds(pl.multiple_of(x * 32, 32), 32), :] + x_recv[0] + x_recv[1] + x_recv[2]
    )
    zr = send(
        r_own.at[pl.ds(pl.multiple_of((1 - zh) * 16, 16), 16), :],
        z_recv,
        s_z.at[1],
        r_z.at[1],
        zdev[4],
    )
    zr.wait_recv()
    code_val = (r_own[pl.ds(pl.multiple_of(zh * 16, 16), 16), :] + z_recv[...]).astype(BF16)
    code_sh[...] = jnp.where(y == 3, jnp.zeros_like(code_val), code_val)
    cz = [
        send(code_sh, code.at[x, slab, own_half], s_z.at[2 + k], r_z.at[2 + k], updev[k])
        for k in range(8)
    ]
    sz = [
        send(st_sh, st.at[x, slab, own_half], s_z.at[10 + k], r_z.at[10 + k], zdev[k])
        for k in range(1, 8)
    ]
    si = [
        send(stin_h.at[0], stin_v.at[dp], s_z.at[17 + k], r_z.at[17 + k], dpdev[k])
        for k in range(1, 4)
    ]

    wz.wait_recv()
    far_w = w_all.at[(1 - zh) * 4 + x, :, own_lane]
    wx2 = [send(far_w, far_w, s_x.at[13 + k], r_x.at[13 + k], xdev[k]) for k in range(1, 4)]
    wc.append(send(far_w, far_w, s_core.at[3], r_core.at[3], sib))

    for cp in ga_in:
        cp.wait_recv()
    l_ga.wait()
    gac = send(ga.at[c], ga.at[c], s_core.at[10], r_core.at[10], sib)

    def gather_x(buf, base):
        src = buf.at[x, :, own_half]
        return [send(src, src, s_x.at[base + k], r_x.at[base + k], xdev[k]) for k in range(1, 4)]

    def to_sibling(buf, slot, i):
        src = buf.at[slot, :, own_half]
        return send(src, src, s_core.at[i], r_core.at[i], sib)

    for cp in cz:
        cp.wait_recv()
    cc = [to_sibling(code, x, 11)]
    cx = gather_x(code, 16)
    for cp in sz:
        cp.wait_recv()
    sc = [to_sibling(st, x, 15)]
    sx = gather_x(st, 19)

    for k in range(1, 4):
        wx[k - 1].wait_recv()
        ref = w_all.at[zh * 4 + xs[4 - k], :, own_lane]
        wc.append(send(ref, ref, s_core.at[3 + k], r_core.at[3 + k], sib))
    for k in range(1, 4):
        cx[k - 1].wait_recv()
        cc.append(to_sibling(code, xs[4 - k], 11 + k))
    for k in range(1, 4):
        wx2[k - 1].wait_recv()
        ref = w_all.at[(1 - zh) * 4 + xs[4 - k], :, own_lane]
        wc.append(send(ref, ref, s_core.at[6 + k], r_core.at[6 + k], sib))
    for cp in wc:
        cp.wait_recv()

    gac.wait_recv()
    l_dec.wait()
    pb[...] = jnp.zeros_like(pb)

    def back(j, carry):
        lanes = pl.ds(pl.multiple_of(j * 128, 128), 128)
        g = jnp.concatenate(
            [ga[0, :, :, lanes].reshape(64, 128), ga[1, :, :, lanes].reshape(64, 128)], axis=1
        )
        part = lax.dot_general(g, w_all[j, own_half, :], LAST, preferred_element_type=F32)
        pb[...] += part.reshape(4, 16, 512)
        return carry

    lax.fori_loop(0, 8, back, 0)
    pr = [
        send(pb.at[(dp + k) % 4], pb_r.at[k - 1], s_z.at[20 + k], r_z.at[20 + k], dpdev[k])
        for k in range(1, 4)
    ]

    l_gain.wait()
    for cp in l_gu:
        cp.wait()
    lane_id = lax.broadcasted_iota(jnp.int32, (128, 128), 1)
    ssq[...] = jnp.zeros_like(ssq)
    gus = []
    own_m = pl.ds(pl.multiple_of(dp * 32, 32), 32)

    def group(k):
        slot = xs[(4 - k) % 4]
        cc[k].wait_recv()
        acc[...] = jnp.zeros_like(acc)

        def decode(j, carry):
            dec = jnp.dot(code[slot], w_all[j], preferred_element_type=F32)
            dec = dec.astype(BF16).astype(F32)
            cols = pl.ds(pl.multiple_of(j * 256, 256), 256)
            normed[:, cols] = (dec * gain_v[:, cols]).astype(BF16)
            sq = dec * dec
            acc[:, 0:128] += sq[:, :128] + sq[:, 128:]
            return carry

        lax.fori_loop(0, 8, decode, 0)
        total = jnp.sum(acc[:, 0:128], axis=1, keepdims=True)
        ssq[...] += jnp.where(lane_id == k, total, 0.0).reshape(4, 32, 128)

        def project(n, carry):
            v = jnp.dot(normed[...], wgu[n], preferred_element_type=F32)
            acc[...] = v
            gu_s[k, :, n] = v.astype(BF16).reshape(4, 32, 256)
            gu_own[k, n] = acc[own_m, :]
            return carry

        lax.fori_loop(0, 7, project, 0)
        for q in range(1, 4):
            gus.append(
                send(
                    gu_s.at[k, (dp + q) % 4],
                    gu_r.at[k, q - 1],
                    s_gu.at[k * 3 + q - 1],
                    r_gu.at[k * 3 + q - 1],
                    dpdev[q],
                )
            )

    group(0)
    for cp in pr:
        cp.wait_recv()
    cg = (pb[dp] + pb_r[0] + pb_r[1] + pb_r[2]).astype(BF16)
    cg_sh[...] = jnp.where(y == 0, jnp.zeros_like(cg), cg)
    rz = [
        send(cg_sh, ret.at[x, slab, own_half], s_z.at[24 + k], r_z.at[24 + k], downdev[k])
        for k in range(8)
    ]
    group(1)
    group(2)
    group(3)
    sq_in = [
        send(ssq.at[(dp + q) % 4], ssq_r.at[q - 1], s_gu.at[11 + q], r_gu.at[11 + q], dpdev[q])
        for q in range(1, 4)
    ]

    for cp in rz:
        cp.wait_recv()
    rc = [to_sibling(ret, x, 19)]
    rx = gather_x(ret, 22)

    for k in range(1, 4):
        sx[k - 1].wait_recv()
        sc.append(to_sibling(st, xs[4 - k], 15 + k))
    l_grad.wait()
    for cp in sc:
        cp.wait_recv()
    grads = grad_v[...].reshape(4, 2, 4, 16, 128)
    perm = jnp.concatenate([grads[:, :, v].reshape(128, 128) for v in range(4)], axis=0)
    for h in range(4):
        cols = pl.ds(h * 256, 256)
        lhs = st[:, :, cols].reshape(512, 256)
        decg_o[0, cols, :] = lax.dot_general(lhs, perm, FIRST, preferred_element_type=F32)

    for k in range(1, 4):
        rx[k - 1].wait_recv()
        rc.append(to_sibling(ret, xs[4 - k], 19 + k))
    for cp in rc:
        cp.wait_recv()
    l_stin.wait()
    for cp in si:
        cp.wait_recv()
    for v in range(4):
        own_ret = ret[v, own_m, :]
        ing_o[0, pl.ds(v * 32, 32), :] = lax.dot_general(
            own_ret, enc_v[...], LAST, preferred_element_type=F32
        ).astype(BF16)
    rhs = ret[:, :, pl.ds(pl.multiple_of(dp * 256, 256), 256)].reshape(512, 256)
    for h in range(2):
        cols = pl.ds(h * 256, 256)
        lhs = jnp.concatenate(
            [stin_v[:, pl.ds(v * 32, 32), cols].reshape(128, 256) for v in range(4)], axis=0
        )
        encg_o[0, cols, :] = lax.dot_general(lhs, rhs, FIRST, preferred_element_type=F32)

    for cp in sq_in:
        cp.wait_recv()
    total = ssq[dp] + ssq_r[0] + ssq_r[1] + ssq_r[2]
    inv_all = lax.rsqrt(total / D + epsilon)
    for k in range(4):
        for q in range(3):
            gus[k * 3 + q].wait_recv()
        inv = inv_all[:, k : k + 1]
        rows = pl.ds(pl.multiple_of(xs[(4 - k) % 4] * 32, 32), 32)
        for n in range(7):
            s = (
                gu_own[k, n]
                + gu_r[k, 0, n].astype(F32)
                + gu_r[k, 1, n].astype(F32)
                + gu_r[k, 2, n].astype(F32)
            ) * inv
            gate = s[:, :128]
            act = gate / (1.0 + jnp.exp(-gate)) * s[:, 128:]
            act_o[0, rows, pl.ds(n * 128, 128)] = act.astype(BF16)

    for cp in pending:
        cp.wait_send()


def per_device(
    outgoing,
    stashed_inputs,
    encoder,
    decoder,
    norm_gain,
    gate_matrix,
    up_matrix,
    grad_decoded,
    stashed_codes,
):
    grad = grad_decoded.reshape(4, 128, 128)
    anywhere = pl.BlockSpec(memory_space=pl.ANY)
    vmem = pl.BlockSpec(memory_space=pltpu.VMEM)
    V = pltpu.VMEM
    DMA = pltpu.SemaphoreType.DMA
    return pl.pallas_call(
        kernel,
        name="section",
        out_shape=(
            jax.ShapeDtypeStruct((1, 128, 896), BF16),
            jax.ShapeDtypeStruct((1, 128, 512), BF16),
            jax.ShapeDtypeStruct((1, 512, 256), F32),
            jax.ShapeDtypeStruct((1, 1024, 128), F32),
        ),
        in_specs=[anywhere] * 8 + [vmem],
        out_specs=(vmem,) * 4,
        scratch_shapes=[
            V((128, 512), BF16),
            V((512, 1024), BF16),
            V((1, 2048), F32),
            V((4, 128, 128), BF16),
            V((4, 128, 512), BF16),
            V((7, 2048, 256), BF16),
            V((8, 1024, 256), BF16),
            V((128, 512), F32),
            V((128, 512), F32),
            V((128, 512), F32),
            V((3, 32, 512), F32),
            V((32, 512), F32),
            V((16, 512), F32),
            V((16, 512), BF16),
            V((4, 128, 1024), BF16),
            V((16, 512), BF16),
            V((16, 512), BF16),
            V((16, 512), BF16),
            V((4, 128, 1024), BF16),
            V((2, 4, 16, 1024), BF16),
            V((4, 16, 512), F32),
            V((3, 16, 512), F32),
            V((16, 512), BF16),
            V((4, 128, 1024), BF16),
            V((128, 2048), BF16),
            V((128, 256), F32),
            V((4, 4, 7, 32, 256), BF16),
            V((4, 3, 7, 32, 256), BF16),
            V((4, 7, 32, 256), F32),
            V((4, 32, 128), F32),
            V((3, 32, 128), F32),
            DMA((7,)),
            DMA((14,)),
            DMA((23,)),
            DMA((23,)),
            DMA((26,)),
            DMA((26,)),
            DMA((32,)),
            DMA((32,)),
            DMA((15,)),
            DMA((15,)),
        ],
        compiler_params=pltpu.CompilerParams(
            collective_id=0, has_side_effects=True, vmem_limit_bytes=60 * 2**20
        ),
    )(
        outgoing,
        stashed_inputs,
        encoder,
        decoder,
        norm_gain,
        gate_matrix,
        up_matrix,
        grad,
        stashed_codes,
    )


def solution(mesh):
    placed = (
        P("pipe", "dp", "tensor"),
        P("pipe", "dp", "tensor"),
        P("pipe", "tensor", None),
        P("pipe", None, ("dp", "tensor")),
        P("pipe", "dp"),
        P("pipe", "dp", "tensor"),
        P("pipe", "dp", "tensor"),
        P("pipe", None, ("dp", "tensor")),
        P("pipe", ("dp", "tensor"), None),
    )
    return jax.shard_map(
        per_device,
        mesh=mesh,
        in_specs=placed,
        out_specs=(
            P("pipe", "dp", "tensor"),
            P("pipe", "dp", "tensor"),
            P("pipe", "tensor", "dp"),
            P("pipe", None, ("dp", "tensor")),
        ),
        check_vma=False,
    )
```

```python
import jax
import jax.numpy as jnp
from jax import lax
from jax.experimental import pallas as pl
from jax.experimental.pallas import tpu as pltpu
from jax.sharding import PartitionSpec as P

D = 8192
epsilon = 1e-05
MESH = pl.DeviceIdType.MESH
F32 = jnp.float32
BF16 = jnp.bfloat16

LAST = (((1,), (1,)), ((), ()))
FIRST = (((0,), (0,)), ((), ()))


def kernel(
    out_h,
    stin_h,
    enc_h,
    dec_h,
    gain_h,
    gate_h,
    up_h,
    grad_h,
    stc_v,
    act_o,
    ing_o,
    encg_o,
    decg_o,
    out_v,
    enc_v,
    gain_v,
    grad_v,
    stin_v,
    wgu,
    w_all,
    q_send,
    q_recv,
    q_own,
    x_recv,
    r_own,
    z_recv,
    code_sh,
    code,
    blk,
    blk_r,
    st_sh,
    st,
    ga,
    pb,
    pb_r,
    cg_sh,
    ret,
    normed,
    acc,
    gu_s,
    gu_r,
    gu_own,
    gu_far,
    ssq,
    ssq_r,
    local_sem,
    wload_sem,
    s_core,
    r_core,
    s_x,
    r_x,
    s_z,
    r_z,
    s_gu,
    r_gu,
):
    dp = lax.axis_index("dp")
    y = lax.axis_index("pipe")
    t = lax.axis_index("tensor")
    zh = t // 8
    x = (t // 2) % 4
    c = t % 2
    z = zh * 4 + dp

    def dev(z_, y_, x_, c_):
        return (z_ % 4, y_, (z_ // 4) * 8 + x_ * 2 + c_)

    sib = dev(z, y, x, 1 - c)
    xs = [(x + k) % 4 for k in range(4)]
    xdev = [dev(z, y, v, c) for v in xs]
    zdev = [dev((z + k) % 8, y, x, c) for k in range(8)]
    updev = [dev((z + k) % 8, (y + 1) % 4, x, c) for k in range(8)]
    downdev = [dev((z + k) % 8, (y + 3) % 4, x, c) for k in range(8)]
    far = [dev((z + 4) % 8, y, v, c) for v in xs]
    dpdev = [((dp + k) % 4, y, t) for k in range(4)]

    def half(c_):
        return pl.ds(pl.multiple_of(c_ * 512, 512), 512)

    own_half = half(c)
    own_lane = pl.ds(pl.multiple_of(c * 128, 128), 128)
    slab = pl.ds(pl.multiple_of((dp * 2 + zh) * 16, 16), 16)

    pending = []

    def send(src, dst, ss, rs, to):
        cp = pltpu.make_async_remote_copy(
            src_ref=src, dst_ref=dst, send_sem=ss, recv_sem=rs, device_id=to, device_id_type=MESH
        )
        cp.start()
        pending.append(cp)
        return cp

    def local(src, dst, sem):
        cp = pltpu.make_async_copy(src, dst, sem)
        cp.start()
        return cp

    l_out = local(out_h.at[0], out_v, local_sem.at[0])
    l_enc = local(enc_h.at[0], enc_v, local_sem.at[1])
    own_w = w_all.at[zh * 4 + x, :, own_lane]
    l_dec = local(dec_h.at[0], own_w, local_sem.at[2])
    own_slot = pl.ds(pl.multiple_of((zh * 4 + x) * 128, 128), 128)
    own_rows = pl.ds(pl.multiple_of(x * 32 + zh * 16, 16), 16)
    l_ga = local(grad_h.at[:, own_rows, :], ga.at[c, :, :, own_slot], local_sem.at[3])
    l_grad = local(grad_h, grad_v, local_sem.at[4])
    l_gain = local(gain_h, gain_v, local_sem.at[5])
    l_stin = local(stin_h.at[0], stin_v.at[dp], local_sem.at[6])
    l_gu = []
    for n in range(7):
        cols = pl.ds(n * 128, 128)
        l_gu.append(local(gate_h.at[0, :, cols], wgu.at[n, :, pl.ds(0, 128)], wload_sem.at[2 * n]))
        l_gu.append(local(up_h.at[0, :, cols], wgu.at[n, :, pl.ds(128, 128)], wload_sem.at[2 * n + 1]))

    barrier = pltpu.get_barrier_semaphore()
    peers = [sib] + xdev[1:] + zdev[1:] + updev + downdev + far[1:]
    for p in peers:
        pl.semaphore_signal(barrier, inc=1, device_id=p, device_id_type=MESH)
    pl.semaphore_wait(barrier, len(peers))

    top, bottom = pl.ds(0, 512), pl.ds(512, 512)
    halves = (top, bottom)

    def w_part(j, rows):
        return w_all.at[j, rows, own_lane]

    near_j = zh * 4
    far_j = (1 - zh) * 4
    wz = [
        send(dec_h.at[0, rows, :], w_part(near_j + x, rows), s_z.at[i], r_z.at[i], zdev[4])
        for i, rows in ((0, top), (32, bottom))
    ]
    ga_in = []
    for k in range(4):
        for h in range(2):
            if k == 0 and h == 0:
                continue
            zh_to = (zh + h) % 2
            rows = pl.ds(pl.multiple_of(xs[k] * 32 + zh_to * 16, 16), 16)
            to = far[k] if h else xdev[k]
            i = k * 2 + h
            ga_in.append(
                send(grad_h.at[:, rows, :], ga.at[c, :, :, own_slot], s_x.at[i], r_x.at[i], to)
            )

    l_out.wait()
    l_enc.wait()
    q_send[...] = jnp.dot(out_v[...], enc_v[:, half(1 - c)], preferred_element_type=F32)
    qc = send(q_send, q_recv, s_core.at[0], r_core.at[0], sib)
    stc = stc_v[0].astype(F32)
    blk[...] = jnp.concatenate([stc[:, :512], stc[:, 512:]], axis=0).astype(BF16)
    bc = send(blk, blk_r, s_core.at[1], r_core.at[1], sib)
    q_own[...] = jnp.dot(out_v[...], enc_v[:, own_half], preferred_element_type=F32)
    qc.wait_recv()
    q_own[...] += q_recv[...]
    xr = []
    for k in range(1, 4):
        rows = pl.ds(pl.multiple_of(xs[k] * 32, 32), 32)
        xr.append(send(q_own.at[rows, :], x_recv.at[k - 1], s_x.at[7 + k], r_x.at[7 + k], xdev[k]))
    wx = {}
    for k, h in ((1, 0), (3, 1), (1, 1), (3, 0)):
        i = 11 + (k // 2) * 2 + h
        rows = halves[h]
        wx[k, h] = send(
            dec_h.at[0, rows, :], w_part(near_j + x, rows), s_x.at[i], r_x.at[i], xdev[k]
        )
    wc = [send(dec_h.at[0], own_w, s_core.at[2], r_core.at[2], sib)]

    bc.wait_recv()
    a = blk[...].astype(F32)
    b = blk_r[...].astype(F32)
    mine = jnp.where(c == 0, a[:8], a[8:])
    other = jnp.where(c == 0, b[:8], b[8:])
    first = jnp.where(c == 0, mine, other)
    second = jnp.where(c == 0, other, mine)
    st_val = jnp.concatenate([first, second], axis=0).astype(BF16)
    st_sh[...] = st_val
    st[x, slab, own_half] = st_val

    for cp in xr:
        cp.wait_recv()
    r_own[...] = (
        q_own[pl.ds(pl.multiple_of(x * 32, 32), 32), :] + x_recv[0] + x_recv[1] + x_recv[2]
    )
    zr = send(
        r_own.at[pl.ds(pl.multiple_of((1 - zh) * 16, 16), 16), :],
        z_recv,
        s_z.at[1],
        r_z.at[1],
        zdev[4],
    )
    wf = {}

    def far_out(h):
        wz[h].wait_recv()
        src = w_part(far_j + x, halves[h])
        for k in (1, 3):
            i = 15 + (k // 2) * 2 + h
            wf[k, h] = send(src, src, s_x.at[i], r_x.at[i], xdev[k])

    def pass_on(group, j, i):
        group[1, 0].wait_recv()
        src = w_part(j + xs[3], top)
        right = send(src, src, s_x.at[i], r_x.at[i], xdev[1])
        group[3, 1].wait_recv()
        src = w_part(j + xs[1], bottom)
        left = send(src, src, s_x.at[i + 1], r_x.at[i + 1], xdev[3])
        return right, left

    def core_out(j, i):
        src = w_all.at[j, :, own_lane]
        wc.append(send(src, src, s_core.at[i], r_core.at[i], sib))

    far_out(0)
    zr.wait_recv()
    code_val = (r_own[pl.ds(pl.multiple_of(zh * 16, 16), 16), :] + z_recv[...]).astype(BF16)
    code_sh[...] = jnp.where(y == 3, jnp.zeros_like(code_val), code_val)
    cz = [
        send(code_sh, code.at[x, slab, own_half], s_z.at[2 + k], r_z.at[2 + k], updev[k])
        for k in range(8)
    ]
    far_out(1)
    wx_fwd = pass_on(wx, near_j, 19)
    sz = [
        send(st_sh, st.at[x, slab, own_half], s_z.at[10 + k], r_z.at[10 + k], zdev[k])
        for k in range(1, 8)
    ]
    si = [
        send(stin_h.at[0], stin_v.at[dp], s_z.at[17 + k], r_z.at[17 + k], dpdev[k])
        for k in range(1, 4)
    ]
    core_out(far_j + x, 3)
    for cp in ga_in:
        cp.wait_recv()
    l_ga.wait()
    gac = send(ga.at[c], ga.at[c], s_core.at[10], r_core.at[10], sib)
    wx[1, 1].wait_recv()
    core_out(near_j + xs[3], 4)
    wx[3, 0].wait_recv()
    core_out(near_j + xs[1], 5)
    wf_fwd = pass_on(wf, far_j, 21)

    def gather_x(buf, base):
        src = buf.at[x, :, own_half]
        return [send(src, src, s_x.at[base + k], r_x.at[base + k], xdev[k]) for k in range(1, 4)]

    def to_sibling(buf, slot, i):
        src = buf.at[slot, :, own_half]
        return send(src, src, s_core.at[i], r_core.at[i], sib)

    for cp in cz:
        cp.wait_recv()
    cc = [to_sibling(code, x, 11)]
    cx = gather_x(code, 22)
    for cp in wx_fwd:
        cp.wait_recv()
    core_out(near_j + xs[2], 6)
    wf[1, 1].wait_recv()
    core_out(far_j + xs[3], 7)
    wf[3, 0].wait_recv()
    core_out(far_j + xs[1], 8)
    for cp in wf_fwd:
        cp.wait_recv()
    core_out(far_j + xs[2], 9)
    for cp in wc:
        cp.wait_recv()

    gac.wait_recv()
    l_dec.wait()
    pb[...] = jnp.zeros_like(pb)

    def back(j, carry):
        lanes = pl.ds(pl.multiple_of(j * 128, 128), 128)
        g = jnp.concatenate(
            [ga[0, :, :, lanes].reshape(64, 128), ga[1, :, :, lanes].reshape(64, 128)], axis=1
        )
        part = lax.dot_general(g, w_all[j, own_half, :], LAST, preferred_element_type=F32)
        pb[...] += part.reshape(4, 16, 512)
        return carry

    lax.fori_loop(0, 8, back, 0)
    pr = [
        send(pb.at[(dp + k) % 4], pb_r.at[k - 1], s_z.at[20 + k], r_z.at[20 + k], dpdev[k])
        for k in range(1, 4)
    ]

    l_gain.wait()
    for cp in l_gu:
        cp.wait()
    lane_id = lax.broadcasted_iota(jnp.int32, (128, 128), 1)
    ssq[...] = jnp.zeros_like(ssq)
    own_m = pl.ds(pl.multiple_of(dp * 32, 32), 32)

    is_end = ((dp + 1) // 2 + 1) % 2
    near = 1 + dp % 2
    other_dp = (dp * 3 + 2) % 5
    opp = 3 * (1 - dp // 2)
    third_dp = is_end * near + (1 - is_end) * opp
    third_slot = 1 + 2 * is_end
    far_m = pl.ds(pl.multiple_of(opp * 32, 32), 32)
    parts = ((0, 4), (4, 7))

    def at_dp(v):
        return (v, y, t)

    def gu_at(buf, k, m, h):
        return buf.at[k, m, pl.ds(parts[h][0], parts[h][1] - parts[h][0])]

    def r_in(k, h, slot):
        return r_gu.at[(k * 2 + h) * 4 + slot]

    def third(k, h):
        return pltpu.make_async_remote_copy(
            src_ref=gu_at(gu_s, k, opp, h),
            dst_ref=gu_at(gu_r, k, third_slot, h),
            send_sem=s_gu.at[(k * 2 + h) * 3 + 2],
            recv_sem=r_in(k, h, third_slot),
            device_id=at_dp(third_dp),
            device_id_type=MESH,
        )

    def wait_in(k, h, slot):
        ref = gu_at(gu_r, k, slot, h)
        pltpu.make_async_remote_copy(
            src_ref=ref,
            dst_ref=ref,
            send_sem=s_gu.at[0],
            recv_sem=r_in(k, h, slot),
            device_id=dpdev[1],
            device_id_type=MESH,
        ).wait_recv()

    def group(k):
        slot = xs[(4 - k) % 4]
        cc[k].wait_recv()
        acc[...] = jnp.zeros_like(acc)

        def decode(j, carry):
            dec = jnp.dot(code[slot], w_all[j], preferred_element_type=F32)
            dec = dec.astype(BF16).astype(F32)
            cols = pl.ds(pl.multiple_of(j * 256, 256), 256)
            normed[:, cols] = (dec * gain_v[:, cols]).astype(BF16)
            sq = dec * dec
            acc[:, 0:128] += sq[:, :128] + sq[:, 128:]
            return carry

        lax.fori_loop(0, 8, decode, 0)
        total = jnp.sum(acc[:, 0:128], axis=1, keepdims=True)
        ssq[...] += jnp.where(lane_id == k, total, 0.0).reshape(4, 32, 128)

        def project(n, carry):
            v = jnp.dot(normed[...], wgu[n], preferred_element_type=F32)
            acc[...] = v
            gu_s[k, :, n] = v.astype(BF16).reshape(4, 32, 256)
            gu_own[k, n] = acc[own_m, :]
            gu_far[k, n] = acc[far_m, :]
            return carry

        for h in range(2):
            lax.fori_loop(parts[h][0], parts[h][1], project, 0)
            i = (k * 2 + h) * 3

            @pl.when(is_end == 1)
            def _():
                third(k, h).start()

            send(gu_at(gu_s, k, near, h), gu_at(gu_r, k, is_end, h), s_gu.at[i], r_in(k, h, is_end), at_dp(near))
            send(
                gu_at(gu_s, k, other_dp, h),
                gu_at(gu_r, k, 2 * is_end, h),
                s_gu.at[i + 1],
                r_in(k, h, 2 * is_end),
                at_dp(other_dp),
            )

    def merge(k):
        @pl.when(is_end == 0)
        def _():
            for h in range(2):
                wait_in(k, h, 3)
                n = pl.ds(parts[h][0], parts[h][1] - parts[h][0])
                gu_s[k, opp, n] = (gu_far[k, n] + gu_r[k, 3, n].astype(F32)).astype(BF16)
                third(k, h).start()

    group(0)
    for k in range(1, 4):
        cx[k - 1].wait_recv()
        cc.append(to_sibling(code, xs[4 - k], 11 + k))
    for cp in pr:
        cp.wait_recv()
    cg = (pb[dp] + pb_r[0] + pb_r[1] + pb_r[2]).astype(BF16)
    cg_sh[...] = jnp.where(y == 0, jnp.zeros_like(cg), cg)
    rz = [
        send(cg_sh, ret.at[x, slab, own_half], s_z.at[24 + k], r_z.at[24 + k], downdev[k])
        for k in range(8)
    ]
    group(1)
    merge(0)
    for cp in sz:
        cp.wait_recv()
    sc = [to_sibling(st, x, 15)]
    sx = gather_x(st, 25)
    group(2)
    merge(1)
    group(3)
    sq_in = [
        send(ssq.at[(dp + q) % 4], ssq_r.at[q - 1], s_gu.at[23 + q], r_gu.at[31 + q], dpdev[q])
        for q in range(1, 4)
    ]
    merge(2)

    for cp in rz:
        cp.wait_recv()
    rc = [to_sibling(ret, x, 19)]
    rx = gather_x(ret, 28)
    merge(3)

    for k in range(1, 4):
        sx[k - 1].wait_recv()
        sc.append(to_sibling(st, xs[4 - k], 15 + k))
    l_grad.wait()
    for cp in sc:
        cp.wait_recv()
    grads = grad_v[...].reshape(4, 2, 4, 16, 128)
    perm = jnp.concatenate([grads[:, :, v].reshape(128, 128) for v in range(4)], axis=0)
    for h in range(4):
        cols = pl.ds(h * 256, 256)
        lhs = st[:, :, cols].reshape(512, 256)
        decg_o[0, cols, :] = lax.dot_general(lhs, perm, FIRST, preferred_element_type=F32)

    for k in range(1, 4):
        rx[k - 1].wait_recv()
        rc.append(to_sibling(ret, xs[4 - k], 19 + k))
    for cp in rc:
        cp.wait_recv()
    l_stin.wait()
    for cp in si:
        cp.wait_recv()
    for v in range(4):
        own_ret = ret[v, own_m, :]
        ing_o[0, pl.ds(v * 32, 32), :] = lax.dot_general(
            own_ret, enc_v[...], LAST, preferred_element_type=F32
        ).astype(BF16)
    rhs = ret[:, :, pl.ds(pl.multiple_of(dp * 256, 256), 256)].reshape(512, 256)
    for h in range(2):
        cols = pl.ds(h * 256, 256)
        lhs = jnp.concatenate(
            [stin_v[:, pl.ds(v * 32, 32), cols].reshape(128, 256) for v in range(4)], axis=0
        )
        encg_o[0, cols, :] = lax.dot_general(lhs, rhs, FIRST, preferred_element_type=F32)

    for cp in sq_in:
        cp.wait_recv()
    total = ssq[dp] + ssq_r[0] + ssq_r[1] + ssq_r[2]
    inv_all = lax.rsqrt(total / D + epsilon)
    for k in range(4):
        for h in range(2):
            wait_in(k, h, 0)
            wait_in(k, h, 1)

        @pl.when(is_end == 0)
        def _():
            for h in range(2):
                wait_in(k, h, 2)
            gu_own[k] += gu_r[k, 2].astype(F32)

        inv = inv_all[:, k : k + 1]
        rows = pl.ds(pl.multiple_of(xs[(4 - k) % 4] * 32, 32), 32)
        for n in range(7):
            s = (
                gu_own[k, n]
                + gu_r[k, 0, n].astype(F32)
                + gu_r[k, 1, n].astype(F32)
            ) * inv
            gate = s[:, :128]
            act = gate / (1.0 + jnp.exp(-gate)) * s[:, 128:]
            act_o[0, rows, pl.ds(n * 128, 128)] = act.astype(BF16)

    for cp in pending:
        cp.wait_send()
    for k in range(4):
        for h in range(2):
            third(k, h).wait_send()


def hand_over(a, b, c, d, a_o, b_o, c_o, d_o, a_v, b_v, c_v, d_v, sem):
    steps = ((c, c_v, c_o), (d, d_v, d_o), (a, a_v, a_o), (b, b_v, b_o))
    loads = [pltpu.make_async_copy(src, via, sem.at[i]) for i, (src, via, _) in enumerate(steps)]
    stores = [
        pltpu.make_async_copy(via, dst, sem.at[4 + i]) for i, (_, via, dst) in enumerate(steps)
    ]
    for cp in loads:
        cp.start()
    for load, store in zip(loads, stores):
        load.wait()
        store.start()
    for cp in stores:
        cp.wait()


def per_device(
    outgoing,
    stashed_inputs,
    encoder,
    decoder,
    norm_gain,
    gate_matrix,
    up_matrix,
    grad_decoded,
    stashed_codes,
):
    grad = grad_decoded.reshape(4, 128, 128)
    anywhere = pl.BlockSpec(memory_space=pl.ANY)
    vmem = pl.BlockSpec(memory_space=pltpu.VMEM)
    V = pltpu.VMEM
    DMA = pltpu.SemaphoreType.DMA
    shapes = (
        jax.ShapeDtypeStruct((1, 128, 896), BF16),
        jax.ShapeDtypeStruct((1, 128, 512), BF16),
        jax.ShapeDtypeStruct((1, 512, 256), F32),
        jax.ShapeDtypeStruct((1, 1024, 128), F32),
    )
    results = pl.pallas_call(
        kernel,
        name="section",
        out_shape=shapes,
        in_specs=[anywhere] * 8 + [vmem],
        out_specs=(vmem,) * 4,
        scratch_shapes=[
            V((128, 512), BF16),
            V((512, 1024), BF16),
            V((1, 2048), F32),
            V((4, 128, 128), BF16),
            V((4, 128, 512), BF16),
            V((7, 2048, 256), BF16),
            V((8, 1024, 256), BF16),
            V((128, 512), F32),
            V((128, 512), F32),
            V((128, 512), F32),
            V((3, 32, 512), F32),
            V((32, 512), F32),
            V((16, 512), F32),
            V((16, 512), BF16),
            V((4, 128, 1024), BF16),
            V((16, 512), BF16),
            V((16, 512), BF16),
            V((16, 512), BF16),
            V((4, 128, 1024), BF16),
            V((2, 4, 16, 1024), BF16),
            V((4, 16, 512), F32),
            V((3, 16, 512), F32),
            V((16, 512), BF16),
            V((4, 128, 1024), BF16),
            V((128, 2048), BF16),
            V((128, 256), F32),
            V((4, 4, 7, 32, 256), BF16),
            V((4, 4, 7, 32, 256), BF16),
            V((4, 7, 32, 256), F32),
            V((4, 7, 32, 256), F32),
            V((4, 32, 128), F32),
            V((3, 32, 128), F32),
            DMA((7,)),
            DMA((14,)),
            DMA((23,)),
            DMA((23,)),
            DMA((32,)),
            DMA((32,)),
            DMA((33,)),
            DMA((33,)),
            DMA((27,)),
            DMA((35,)),
        ],
        compiler_params=pltpu.CompilerParams(
            collective_id=0, has_side_effects=True, vmem_limit_bytes=60 * 2**20
        ),
    )(
        outgoing,
        stashed_inputs,
        encoder,
        decoder,
        norm_gain,
        gate_matrix,
        up_matrix,
        grad,
        stashed_codes,
    )
    return pl.pallas_call(
        hand_over,
        name="hand_over",
        out_shape=shapes,
        in_specs=[anywhere] * 4,
        out_specs=(anywhere,) * 4,
        scratch_shapes=[V(s.shape, s.dtype) for s in shapes] + [DMA((8,))],
        compiler_params=pltpu.CompilerParams(vmem_limit_bytes=60 * 2**20),
    )(*results)


def solution(mesh):
    placed = (
        P("pipe", "dp", "tensor"),
        P("pipe", "dp", "tensor"),
        P("pipe", "tensor", None),
        P("pipe", None, ("dp", "tensor")),
        P("pipe", "dp"),
        P("pipe", "dp", "tensor"),
        P("pipe", "dp", "tensor"),
        P("pipe", None, ("dp", "tensor")),
        P("pipe", ("dp", "tensor"), None),
    )
    return jax.shard_map(
        per_device,
        mesh=mesh,
        in_specs=placed,
        out_specs=(
            P("pipe", "dp", "tensor"),
            P("pipe", "dp", "tensor"),
            P("pipe", "tensor", "dp"),
            P("pipe", None, ("dp", "tensor")),
        ),
        check_vma=False,
    )
```

```python
import jax
import jax.numpy as jnp
from jax import lax
from jax.experimental import pallas as pl
from jax.experimental.pallas import tpu as pltpu
from jax.sharding import PartitionSpec as P

D = 8192
epsilon = 1e-05
MESH = pl.DeviceIdType.MESH
F32 = jnp.float32
BF16 = jnp.bfloat16

LAST = (((1,), (1,)), ((), ()))
FIRST = (((0,), (0,)), ((), ()))


def kernel(
    out_h,
    stin_h,
    enc_h,
    dec_h,
    gain_h,
    gate_h,
    up_h,
    grad_h,
    stc_v,
    act_o,
    ing_o,
    encg_o,
    decg_o,
    out_v,
    enc_v,
    gain_v,
    grad_v,
    stin_v,
    wgu,
    w_all,
    q_send,
    q_recv,
    q_own,
    x_recv,
    r_own,
    z_recv,
    code_sh,
    code,
    blk,
    blk_r,
    st_sh,
    st,
    ga,
    pb,
    pb_s,
    pb_r,
    cg_sh,
    ret,
    dec_s,
    dfar,
    normed,
    acc,
    gu_s,
    gu_r,
    gu_own,
    gu_far,
    ssq,
    ssq_r,
    local_sem,
    wload_sem,
    s_core,
    r_core,
    s_x,
    r_x,
    s_z,
    r_z,
    s_gu,
    r_gu,
):
    dp = lax.axis_index("dp")
    y = lax.axis_index("pipe")
    t = lax.axis_index("tensor")
    zh = t // 8
    x = (t // 2) % 4
    c = t % 2
    z = zh * 4 + dp

    def dev(z_, y_, x_, c_):
        return (z_ % 4, y_, (z_ // 4) * 8 + x_ * 2 + c_)

    sib = dev(z, y, x, 1 - c)
    xs = [(x + k) % 4 for k in range(4)]
    xdev = [dev(z, y, v, c) for v in xs]
    zdev = [dev((z + k) % 8, y, x, c) for k in range(8)]
    updev = [dev((z + k) % 8, (y + 1) % 4, x, c) for k in range(8)]
    downdev = [dev((z + k) % 8, (y + 3) % 4, x, c) for k in range(8)]
    dpdev = [((dp + k) % 4, y, t) for k in range(4)]

    def half(c_):
        return pl.ds(pl.multiple_of(c_ * 512, 512), 512)

    own_half = half(c)
    own_lane = pl.ds(pl.multiple_of(c * 128, 128), 128)
    slab = pl.ds(pl.multiple_of((dp * 2 + zh) * 16, 16), 16)

    pending = []

    def send(src, dst, ss, rs, to):
        cp = pltpu.make_async_remote_copy(
            src_ref=src, dst_ref=dst, send_sem=ss, recv_sem=rs, device_id=to, device_id_type=MESH
        )
        cp.start()
        pending.append(cp)
        return cp

    def local(src, dst, sem):
        cp = pltpu.make_async_copy(src, dst, sem)
        cp.start()
        return cp

    barrier = pltpu.get_barrier_semaphore()
    peers = [sib] + xdev[1:] + zdev[1:] + updev + downdev
    for p in peers:
        pl.semaphore_signal(barrier, inc=1, device_id=p, device_id_type=MESH)

    l_out = local(out_h.at[0], out_v, local_sem.at[0])
    l_enc = local(enc_h.at[0], enc_v, local_sem.at[1])
    own_w = w_all.at[x, :, own_lane]
    l_dec = local(dec_h.at[0], own_w, local_sem.at[2])
    own_slot = pl.ds(pl.multiple_of(x * 128, 128), 128)
    own_rows = pl.ds(pl.multiple_of(x * 32, 32), 32)
    l_ga = local(grad_h.at[:, own_rows, :], ga.at[c, :, :, own_slot], local_sem.at[3])
    l_grad = local(grad_h, grad_v, local_sem.at[4])
    l_gain = local(gain_h, gain_v, local_sem.at[5])
    l_stin = local(stin_h.at[0], stin_v.at[dp], local_sem.at[6])
    l_gu = [
        local(gate_h.at[0], wgu.at[0], wload_sem.at[0]),
        local(up_h.at[0], wgu.at[1], wload_sem.at[1]),
    ]

    l_out.wait()
    l_enc.wait()
    q_send[...] = jnp.dot(out_v[...], enc_v[:, half(1 - c)], preferred_element_type=F32)
    q_own[...] = jnp.dot(out_v[...], enc_v[:, own_half], preferred_element_type=F32)
    stc = stc_v[0].astype(F32)
    blk[...] = jnp.concatenate([stc[:, :512], stc[:, 512:]], axis=0).astype(BF16)
    pl.semaphore_wait(barrier, len(peers))
    qc = send(q_send, q_recv, s_core.at[0], r_core.at[0], sib)
    bc = send(blk, blk_r, s_core.at[1], r_core.at[1], sib)

    si = [
        send(stin_h.at[0], stin_v.at[dp], s_z.at[17 + k], r_z.at[17 + k], dpdev[k])
        for k in range(1, 4)
    ]

    qc.wait_recv()
    q_own[...] += q_recv[...]
    xr = []
    for k in range(1, 4):
        rows = pl.ds(pl.multiple_of(xs[k] * 32, 32), 32)
        xr.append(send(q_own.at[rows, :], x_recv.at[k - 1], s_x.at[7 + k], r_x.at[7 + k], xdev[k]))

    halves = (pl.ds(0, 512), pl.ds(512, 512))
    wx = {}
    for k, h in ((1, 0), (3, 1), (1, 1), (3, 0)):
        i = 11 + (k // 2) * 2 + h
        rows = halves[h]
        wx[k, h] = send(
            dec_h.at[0, rows, :], w_all.at[x, rows, own_lane], s_x.at[i], r_x.at[i], xdev[k]
        )
    wc = [send(dec_h.at[0], own_w, s_core.at[2], r_core.at[2], sib)]

    bc.wait_recv()
    a = blk[...].astype(F32)
    b = blk_r[...].astype(F32)
    mine = jnp.where(c == 0, a[:8], a[8:])
    other = jnp.where(c == 0, b[:8], b[8:])
    first = jnp.where(c == 0, mine, other)
    second = jnp.where(c == 0, other, mine)
    st_val = jnp.concatenate([first, second], axis=0).astype(BF16)
    st_sh[...] = st_val
    st[x, slab, own_half] = st_val

    ga_in = []
    for k in range(1, 4):
        rows = pl.ds(pl.multiple_of(xs[k] * 32, 32), 32)
        ga_in.append(
            send(grad_h.at[:, rows, :], ga.at[c, :, :, own_slot], s_x.at[k], r_x.at[k], xdev[k])
        )

    def core_out(slot, i):
        src = w_all.at[slot, :, own_lane]
        wc.append(send(src, src, s_core.at[i], r_core.at[i], sib))

    def gather_x(buf, base):
        src = buf.at[x, :, own_half]
        return [send(src, src, s_x.at[base + k], r_x.at[base + k], xdev[k]) for k in range(1, 4)]

    def to_sibling(buf, slot, i):
        src = buf.at[slot, :, own_half]
        return send(src, src, s_core.at[i], r_core.at[i], sib)

    for cp in xr:
        cp.wait_recv()
    r_own[...] = (
        q_own[pl.ds(pl.multiple_of(x * 32, 32), 32), :] + x_recv[0] + x_recv[1] + x_recv[2]
    )
    zr = send(
        r_own.at[pl.ds(pl.multiple_of((1 - zh) * 16, 16), 16), :],
        z_recv,
        s_z.at[1],
        r_z.at[1],
        zdev[4],
    )
    wx[1, 0].wait_recv()
    src = w_all.at[xs[3], halves[0], own_lane]
    wx_fwd = [send(src, src, s_x.at[19], r_x.at[19], xdev[1])]
    wx[3, 1].wait_recv()
    src = w_all.at[xs[1], halves[1], own_lane]
    wx_fwd.append(send(src, src, s_x.at[20], r_x.at[20], xdev[3]))

    zr.wait_recv()
    code_val = (r_own[pl.ds(pl.multiple_of(zh * 16, 16), 16), :] + z_recv[...]).astype(BF16)
    code_sh[...] = jnp.where(y == 3, jnp.zeros_like(code_val), code_val)
    cz = [
        send(code_sh, code.at[x, slab, own_half], s_z.at[2 + k], r_z.at[2 + k], updev[k])
        for k in range(8)
    ]
    wx[1, 1].wait_recv()
    core_out(xs[3], 4)
    wx[3, 0].wait_recv()
    core_out(xs[1], 5)
    for cp in ga_in:
        cp.wait_recv()
    l_ga.wait()
    gac = send(ga.at[c], ga.at[c], s_core.at[10], r_core.at[10], sib)
    for cp in wx_fwd:
        cp.wait_recv()
    core_out(xs[2], 6)
    for cp in wc:
        cp.wait_recv()

    gac.wait_recv()
    l_dec.wait()
    for j in range(4):
        lanes = pl.ds(j * 128, 128)
        g = jnp.concatenate(
            [ga[0, :, :, lanes].reshape(128, 128), ga[1, :, :, lanes].reshape(128, 128)], axis=1
        )
        part = lax.dot_general(g, w_all[j, own_half, :], LAST, preferred_element_type=F32)
        if j == 0:
            pb[...] = part
        else:
            pb[...] += part
    pb_s[...] = pb[...].astype(BF16).reshape(8, 16, 512)
    pr = []
    for k in range(1, 8):
        to_z = (z + k) % 8
        src = pb_s.at[(to_z % 4) * 2 + to_z // 4]
        pr.append(send(src, pb_r.at[k - 1], s_z.at[20 + k], r_z.at[20 + k], zdev[k]))

    for cp in cz:
        cp.wait_recv()
    cc = [to_sibling(code, x, 11)]
    cx = gather_x(code, 22)

    l_gain.wait()
    lane_id = lax.broadcasted_iota(jnp.int32, (128, 128), 1)
    ssq[...] = jnp.zeros_like(ssq)

    def scaled(k, dec, col, squares):
        cols = pl.ds(pl.multiple_of(col, 256), 256)
        normed[k, :, cols] = (dec * gain_v[:, cols]).astype(BF16)
        sq = dec * dec
        return squares + sq[:, :128] + sq[:, 128:]

    def add_squares(k, squares):
        total = jnp.sum(squares, axis=1, keepdims=True)
        ssq[...] += jnp.where(lane_id == k, total, 0.0).reshape(4, 32, 128)

    def near_half(k):
        slot = xs[(4 - k) % 4]
        cc[k].wait_recv()
        squares = jnp.zeros((128, 128), F32)
        for i in range(4):
            j = (2 * c + i) % 4
            dec = jnp.dot(code[slot], w_all[j], preferred_element_type=F32).astype(BF16)
            if k == 0 and i < 2:
                dec_s[:, pl.ds(i * 256, 256)] = dec
            if k == 0 and i == 1:
                dz.append(send(dec_s, dfar.at[x, :, own_half], s_z.at[0], r_z.at[0], zdev[4]))
            squares = scaled(k, dec.astype(F32), zh * 1024 + j * 256, squares)
        add_squares(k, squares)

    dz = []
    near_half(0)
    for cp in pr:
        cp.wait_recv()
    cg = pb[slab, :]
    for k in range(7):
        cg += pb_r[k].astype(F32)
    cg = cg.astype(BF16)
    cg_sh[...] = jnp.where(y == 0, jnp.zeros_like(cg), cg)
    rz = [
        send(cg_sh, ret.at[x, slab, own_half], s_z.at[28 + k], r_z.at[28 + k], downdev[k])
        for k in range(8)
    ]
    sz = [
        send(st_sh, st.at[x, slab, own_half], s_z.at[10 + k], r_z.at[10 + k], zdev[k])
        for k in range(1, 8)
    ]
    for k in range(1, 4):
        cx[k - 1].wait_recv()
        cc.append(to_sibling(code, xs[4 - k], 11 + k))
    for k in range(1, 4):
        near_half(k)
    dz[0].wait_recv()
    dc = [to_sibling(dfar, x, 23)]
    dx = gather_x(dfar, 32)

    for cp in l_gu:
        cp.wait()
    own_m = pl.ds(pl.multiple_of(dp * 32, 32), 32)

    is_end = ((dp + 1) // 2 + 1) % 2
    near = 1 + dp % 2
    other_dp = (dp * 3 + 2) % 5
    opp = 3 * (1 - dp // 2)
    third_dp = is_end * near + (1 - is_end) * opp
    third_slot = 1 + 2 * is_end
    far_m = pl.ds(pl.multiple_of(opp * 32, 32), 32)

    def at_dp(v):
        return (v, y, t)

    def r_in(k, h, slot):
        return r_gu.at[(k * 2 + h) * 4 + slot]

    def third(k, h):
        return pltpu.make_async_remote_copy(
            src_ref=gu_s.at[k, h, opp],
            dst_ref=gu_r.at[k, h, third_slot],
            send_sem=s_gu.at[(k * 2 + h) * 3 + 2],
            recv_sem=r_in(k, h, third_slot),
            device_id=at_dp(third_dp),
            device_id_type=MESH,
        )

    def wait_in(k, h, slot):
        ref = gu_r.at[k, h, slot]
        pltpu.make_async_remote_copy(
            src_ref=ref,
            dst_ref=ref,
            send_sem=s_gu.at[0],
            recv_sem=r_in(k, h, slot),
            device_id=dpdev[1],
            device_id_type=MESH,
        ).wait_recv()

    def group(k):
        slot = xs[(4 - k) % 4]
        dc[k].wait_recv()
        squares = jnp.zeros((128, 128), F32)
        for j in range(4):
            dec = dfar[slot, :, pl.ds(j * 256, 256)].astype(F32)
            squares = scaled(k, dec, (1 - zh) * 1024 + j * 256, squares)
        add_squares(k, squares)

        for h in range(2):
            v = jnp.dot(normed[k], wgu[h], preferred_element_type=F32)
            acc[...] = v
            gu_s[k, h] = v.astype(BF16).reshape(4, 32, 896)
            i = (k * 2 + h) * 3

            @pl.when(is_end == 1)
            def _():
                third(k, h).start()

            send(gu_s.at[k, h, near], gu_r.at[k, h, is_end], s_gu.at[i], r_in(k, h, is_end), at_dp(near))
            send(
                gu_s.at[k, h, other_dp],
                gu_r.at[k, h, 2 * is_end],
                s_gu.at[i + 1],
                r_in(k, h, 2 * is_end),
                at_dp(other_dp),
            )
            gu_own[k, h] = acc[own_m, :]
            gu_far[k, h] = acc[far_m, :]

    def merge(k):
        @pl.when(is_end == 0)
        def _():
            for h in range(2):
                wait_in(k, h, 3)
                gu_s[k, h, opp] = (gu_far[k, h] + gu_r[k, h, 3].astype(F32)).astype(BF16)
                third(k, h).start()

    group(0)
    for k in range(1, 4):
        dx[k - 1].wait_recv()
        dc.append(to_sibling(dfar, xs[4 - k], 23 + k))
    group(1)
    merge(0)
    for cp in rz:
        cp.wait_recv()
    rc = [to_sibling(ret, x, 19)]
    rx = gather_x(ret, 28)
    group(2)
    merge(1)
    group(3)
    sq_in = [
        send(ssq.at[(dp + q) % 4], ssq_r.at[q - 1], s_gu.at[23 + q], r_gu.at[31 + q], dpdev[q])
        for q in range(1, 4)
    ]
    for cp in sz:
        cp.wait_recv()
    sc = [to_sibling(st, x, 15)]
    sx = gather_x(st, 25)
    merge(2)
    merge(3)

    for k in range(1, 4):
        sx[k - 1].wait_recv()
        sc.append(to_sibling(st, xs[4 - k], 15 + k))
    l_grad.wait()
    for cp in sc:
        cp.wait_recv()
    grads = grad_v[...].reshape(4, 2, 4, 16, 128)
    perm = jnp.concatenate([grads[:, :, v].reshape(128, 128) for v in range(4)], axis=0)
    for h in range(4):
        cols = pl.ds(h * 256, 256)
        lhs = st[:, :, cols].reshape(512, 256)
        decg_o[0, cols, :] = lax.dot_general(lhs, perm, FIRST, preferred_element_type=F32)

    for k in range(1, 4):
        rx[k - 1].wait_recv()
        rc.append(to_sibling(ret, xs[4 - k], 19 + k))
    for cp in rc:
        cp.wait_recv()
    l_stin.wait()
    for cp in si:
        cp.wait_recv()
    for v in range(4):
        own_ret = ret[v, own_m, :]
        ing_o[0, pl.ds(v * 32, 32), :] = lax.dot_general(
            own_ret, enc_v[...], LAST, preferred_element_type=F32
        ).astype(BF16)
    rhs = ret[:, :, pl.ds(pl.multiple_of(dp * 256, 256), 256)].reshape(512, 256)
    for h in range(2):
        cols = pl.ds(h * 256, 256)
        lhs = jnp.concatenate(
            [stin_v[:, pl.ds(v * 32, 32), cols].reshape(128, 256) for v in range(4)], axis=0
        )
        encg_o[0, cols, :] = lax.dot_general(lhs, rhs, FIRST, preferred_element_type=F32)

    for cp in sq_in:
        cp.wait_recv()
    total = ssq[dp] + ssq_r[0] + ssq_r[1] + ssq_r[2]
    inv_all = lax.rsqrt(total / D + epsilon)
    for k in range(4):
        for h in range(2):
            wait_in(k, h, 0)
            wait_in(k, h, 1)

        @pl.when(is_end == 0)
        def _():
            for h in range(2):
                wait_in(k, h, 2)
                gu_own[k, h] += gu_r[k, h, 2].astype(F32)

        inv = inv_all[:, k : k + 1]
        rows = pl.ds(pl.multiple_of(xs[(4 - k) % 4] * 32, 32), 32)
        gate, up = [
            (gu_own[k, h] + gu_r[k, h, 0].astype(F32) + gu_r[k, h, 1].astype(F32)) * inv
            for h in range(2)
        ]
        act_o[0, rows, :] = (gate / (1.0 + jnp.exp(-gate)) * up).astype(BF16)

    for cp in pending:
        cp.wait_send()
    for k in range(4):
        for h in range(2):
            third(k, h).wait_send()


def hand_over(a, b, c, d, a_o, b_o, c_o, d_o, a_v, b_v, c_v, d_v, sem):
    steps = ((c, c_v, c_o), (d, d_v, d_o), (a, a_v, a_o), (b, b_v, b_o))
    loads = [pltpu.make_async_copy(src, via, sem.at[i]) for i, (src, via, _) in enumerate(steps)]
    stores = [
        pltpu.make_async_copy(via, dst, sem.at[4 + i]) for i, (_, via, dst) in enumerate(steps)
    ]
    for cp in loads:
        cp.start()
    for load, store in zip(loads, stores):
        load.wait()
        store.start()
    for cp in stores:
        cp.wait()


def per_device(
    outgoing,
    stashed_inputs,
    encoder,
    decoder,
    norm_gain,
    gate_matrix,
    up_matrix,
    grad_decoded,
    stashed_codes,
):
    grad = grad_decoded.reshape(4, 128, 128)
    anywhere = pl.BlockSpec(memory_space=pl.ANY)
    vmem = pl.BlockSpec(memory_space=pltpu.VMEM)
    V = pltpu.VMEM
    DMA = pltpu.SemaphoreType.DMA
    shapes = (
        jax.ShapeDtypeStruct((1, 128, 896), BF16),
        jax.ShapeDtypeStruct((1, 128, 512), BF16),
        jax.ShapeDtypeStruct((1, 512, 256), F32),
        jax.ShapeDtypeStruct((1, 1024, 128), F32),
    )
    results = pl.pallas_call(
        kernel,
        name="section",
        out_shape=shapes,
        in_specs=[anywhere] * 8 + [vmem],
        out_specs=(vmem,) * 4,
        scratch_shapes=[
            V((128, 512), BF16),
            V((512, 1024), BF16),
            V((1, 2048), F32),
            V((4, 128, 128), BF16),
            V((4, 128, 512), BF16),
            V((2, 2048, 896), BF16),
            V((4, 1024, 256), BF16),
            V((128, 512), F32),
            V((128, 512), F32),
            V((128, 512), F32),
            V((3, 32, 512), F32),
            V((32, 512), F32),
            V((16, 512), F32),
            V((16, 512), BF16),
            V((4, 128, 1024), BF16),
            V((16, 512), BF16),
            V((16, 512), BF16),
            V((16, 512), BF16),
            V((4, 128, 1024), BF16),
            V((2, 4, 32, 512), BF16),
            V((128, 512), F32),
            V((8, 16, 512), BF16),
            V((7, 16, 512), BF16),
            V((16, 512), BF16),
            V((4, 128, 1024), BF16),
            V((128, 512), BF16),
            V((4, 128, 1024), BF16),
            V((4, 128, 2048), BF16),
            V((128, 896), F32),
            V((4, 2, 4, 32, 896), BF16),
            V((4, 2, 4, 32, 896), BF16),
            V((4, 2, 32, 896), F32),
            V((4, 2, 32, 896), F32),
            V((4, 32, 128), F32),
            V((3, 32, 128), F32),
            DMA((7,)),
            DMA((2,)),
            DMA((27,)),
            DMA((27,)),
            DMA((36,)),
            DMA((36,)),
            DMA((36,)),
            DMA((36,)),
            DMA((27,)),
            DMA((35,)),
        ],
        compiler_params=pltpu.CompilerParams(
            collective_id=0, has_side_effects=True, vmem_limit_bytes=60 * 2**20
        ),
    )(
        outgoing,
        stashed_inputs,
        encoder,
        decoder,
        norm_gain,
        gate_matrix,
        up_matrix,
        grad,
        stashed_codes,
    )
    return pl.pallas_call(
        hand_over,
        name="hand_over",
        out_shape=shapes,
        in_specs=[anywhere] * 4,
        out_specs=(anywhere,) * 4,
        scratch_shapes=[V(s.shape, s.dtype) for s in shapes] + [DMA((8,))],
        compiler_params=pltpu.CompilerParams(vmem_limit_bytes=60 * 2**20),
    )(*results)


def solution(mesh):
    placed = (
        P("pipe", "dp", "tensor"),
        P("pipe", "dp", "tensor"),
        P("pipe", "tensor", None),
        P("pipe", None, ("dp", "tensor")),
        P("pipe", "dp"),
        P("pipe", "dp", "tensor"),
        P("pipe", "dp", "tensor"),
        P("pipe", None, ("dp", "tensor")),
        P("pipe", ("dp", "tensor"), None),
    )
    return jax.shard_map(
        per_device,
        mesh=mesh,
        in_specs=placed,
        out_specs=(
            P("pipe", "dp", "tensor"),
            P("pipe", "dp", "tensor"),
            P("pipe", "tensor", "dp"),
            P("pipe", None, ("dp", "tensor")),
        ),
        check_vma=False,
    )
```

```python
import jax
import jax.numpy as jnp
from jax import lax
from jax.experimental import pallas as pl
from jax.experimental.pallas import tpu as pltpu
from jax.sharding import PartitionSpec as P

D = 8192
epsilon = 1e-05
MESH = pl.DeviceIdType.MESH
F32 = jnp.float32
BF16 = jnp.bfloat16

LAST = (((1,), (1,)), ((), ()))
FIRST = (((0,), (0,)), ((), ()))


def kernel(
    out_h,
    stin_h,
    enc_h,
    dec_h,
    gain_h,
    gate_h,
    up_h,
    grad_h,
    stc_v,
    act_o,
    ing_o,
    encg_o,
    decg_o,
    out_v,
    enc_v,
    gain_v,
    grad_v,
    stin_v,
    wgu,
    w_all,
    q_send,
    q_recv,
    q_own,
    x_recv,
    r_own,
    z_recv,
    code_sh,
    code,
    blk,
    blk_r,
    st_sh,
    st,
    ga,
    pb,
    pb_s,
    pb_r,
    cg_sh,
    ret,
    dec_s,
    dfar,
    normed,
    acc,
    gu_s,
    gu_r,
    gu_own,
    gu_far,
    ssq,
    ssq_row,
    ssq_r,
    local_sem,
    wload_sem,
    s_core,
    r_core,
    s_x,
    r_x,
    s_z,
    r_z,
    s_gu,
    r_gu,
):
    dp = lax.axis_index("dp")
    y = lax.axis_index("pipe")
    t = lax.axis_index("tensor")
    zh = t // 8
    x = (t // 2) % 4
    c = t % 2
    z = zh * 4 + dp

    def dev(z_, y_, x_, c_):
        return (z_ % 4, y_, (z_ // 4) * 8 + x_ * 2 + c_)

    sib = dev(z, y, x, 1 - c)
    xs = [(x + k) % 4 for k in range(4)]
    xdev = [dev(z, y, v, c) for v in xs]
    zdev = [dev((z + k) % 8, y, x, c) for k in range(8)]
    updev = [dev((z + k) % 8, (y + 1) % 4, x, c) for k in range(8)]
    downdev = [dev((z + k) % 8, (y + 3) % 4, x, c) for k in range(8)]
    dpdev = [((dp + k) % 4, y, t) for k in range(4)]

    def half(c_):
        return pl.ds(pl.multiple_of(c_ * 512, 512), 512)

    own_half = half(c)
    own_lane = pl.ds(pl.multiple_of(c * 128, 128), 128)
    slab = pl.ds(pl.multiple_of((dp * 2 + zh) * 16, 16), 16)

    pending = []

    def send(src, dst, ss, rs, to):
        cp = pltpu.make_async_remote_copy(
            src_ref=src, dst_ref=dst, send_sem=ss, recv_sem=rs, device_id=to, device_id_type=MESH
        )
        cp.start()
        pending.append(cp)
        return cp

    def local(src, dst, sem):
        cp = pltpu.make_async_copy(src, dst, sem)
        cp.start()
        return cp

    barrier = pltpu.get_barrier_semaphore()
    peers = [sib] + xdev[1:] + zdev[1:] + updev + downdev
    for p in peers:
        pl.semaphore_signal(barrier, inc=1, device_id=p, device_id_type=MESH)

    l_out = local(out_h.at[0], out_v, local_sem.at[0])
    l_enc = local(enc_h.at[0], enc_v, local_sem.at[1])
    own_w = w_all.at[x, :, own_lane]
    l_dec = local(dec_h.at[0], own_w, local_sem.at[2])
    own_slot = pl.ds(pl.multiple_of(x * 128, 128), 128)
    own_rows = pl.ds(pl.multiple_of(x * 32, 32), 32)
    l_ga = local(grad_h.at[:, own_rows, :], ga.at[c, :, :, own_slot], local_sem.at[3])
    l_grad = local(grad_h, grad_v, local_sem.at[4])
    l_gain = local(gain_h, gain_v, local_sem.at[5])
    l_stin = local(stin_h.at[0], stin_v.at[dp], local_sem.at[6])
    l_gu = [
        local(gate_h.at[0], wgu.at[0], wload_sem.at[0]),
        local(up_h.at[0], wgu.at[1], wload_sem.at[1]),
    ]

    l_out.wait()
    l_enc.wait()
    q_send[...] = jnp.dot(out_v[...], enc_v[:, half(1 - c)], preferred_element_type=F32)
    q_own[...] = jnp.dot(out_v[...], enc_v[:, own_half], preferred_element_type=F32)
    stc = stc_v[0].astype(F32)
    blk[...] = jnp.concatenate([stc[:, :512], stc[:, 512:]], axis=0).astype(BF16)
    pl.semaphore_wait(barrier, len(peers))
    qc = send(q_send, q_recv, s_core.at[0], r_core.at[0], sib)
    bc = send(blk, blk_r, s_core.at[1], r_core.at[1], sib)

    si = [
        send(stin_h.at[0], stin_v.at[dp], s_z.at[17 + k], r_z.at[17 + k], dpdev[k])
        for k in range(1, 4)
    ]

    qc.wait_recv()
    q_own[...] += q_recv[...]
    xr = []
    for k in range(1, 4):
        rows = pl.ds(pl.multiple_of(xs[k] * 32, 32), 32)
        xr.append(send(q_own.at[rows, :], x_recv.at[k - 1], s_x.at[7 + k], r_x.at[7 + k], xdev[k]))

    halves = (pl.ds(0, 512), pl.ds(512, 512))
    wx = {}
    for k, h in ((1, 0), (3, 1), (1, 1), (3, 0)):
        i = 11 + (k // 2) * 2 + h
        rows = halves[h]
        wx[k, h] = send(
            dec_h.at[0, rows, :], w_all.at[x, rows, own_lane], s_x.at[i], r_x.at[i], xdev[k]
        )
    wc = [send(dec_h.at[0], own_w, s_core.at[2], r_core.at[2], sib)]

    bc.wait_recv()
    a = blk[...].astype(F32)
    b = blk_r[...].astype(F32)
    mine = jnp.where(c == 0, a[:8], a[8:])
    other = jnp.where(c == 0, b[:8], b[8:])
    first = jnp.where(c == 0, mine, other)
    second = jnp.where(c == 0, other, mine)
    st_val = jnp.concatenate([first, second], axis=0).astype(BF16)
    st_sh[...] = st_val
    st[x, slab, own_half] = st_val

    ga_in = []
    for k in range(1, 4):
        rows = pl.ds(pl.multiple_of(xs[k] * 32, 32), 32)
        ga_in.append(
            send(grad_h.at[:, rows, :], ga.at[c, :, :, own_slot], s_x.at[k], r_x.at[k], xdev[k])
        )

    def core_out(slot, i):
        src = w_all.at[slot, :, own_lane]
        wc.append(send(src, src, s_core.at[i], r_core.at[i], sib))

    def gather_x(buf, base):
        src = buf.at[x, :, own_half]
        return [send(src, src, s_x.at[base + k], r_x.at[base + k], xdev[k]) for k in range(1, 4)]

    def to_sibling(buf, slot, i):
        src = buf.at[slot, :, own_half]
        return send(src, src, s_core.at[i], r_core.at[i], sib)

    for cp in xr:
        cp.wait_recv()
    r_own[...] = (
        q_own[pl.ds(pl.multiple_of(x * 32, 32), 32), :] + x_recv[0] + x_recv[1] + x_recv[2]
    )
    zr = send(
        r_own.at[pl.ds(pl.multiple_of((1 - zh) * 16, 16), 16), :],
        z_recv,
        s_z.at[1],
        r_z.at[1],
        zdev[4],
    )
    wx[1, 0].wait_recv()
    src = w_all.at[xs[3], halves[0], own_lane]
    wx_fwd = [send(src, src, s_x.at[19], r_x.at[19], xdev[1])]
    wx[3, 1].wait_recv()
    src = w_all.at[xs[1], halves[1], own_lane]
    wx_fwd.append(send(src, src, s_x.at[20], r_x.at[20], xdev[3]))

    zr.wait_recv()
    code_val = (r_own[pl.ds(pl.multiple_of(zh * 16, 16), 16), :] + z_recv[...]).astype(BF16)
    code_sh[...] = jnp.where(y == 3, jnp.zeros_like(code_val), code_val)
    cz = [
        send(code_sh, code.at[x, slab, own_half], s_z.at[2 + k], r_z.at[2 + k], updev[k])
        for k in range(8)
    ]
    wx[1, 1].wait_recv()
    core_out(xs[3], 4)
    wx[3, 0].wait_recv()
    core_out(xs[1], 5)
    for cp in ga_in:
        cp.wait_recv()
    l_ga.wait()
    gac = send(ga.at[c], ga.at[c], s_core.at[10], r_core.at[10], sib)
    for cp in wx_fwd:
        cp.wait_recv()
    core_out(xs[2], 6)
    for cp in wc:
        cp.wait_recv()

    gac.wait_recv()
    l_dec.wait()
    for j in range(4):
        lanes = pl.ds(j * 128, 128)
        g = jnp.concatenate(
            [ga[0, :, :, lanes].reshape(128, 128), ga[1, :, :, lanes].reshape(128, 128)], axis=1
        )
        part = lax.dot_general(g, w_all[j, own_half, :], LAST, preferred_element_type=F32)
        if j == 0:
            pb[...] = part
        else:
            pb[...] += part
    pb_s[...] = pb[...].astype(BF16).reshape(8, 16, 512)
    pr = []
    for k in range(1, 8):
        to_z = (z + k) % 8
        src = pb_s.at[(to_z % 4) * 2 + to_z // 4]
        pr.append(send(src, pb_r.at[k - 1], s_z.at[20 + k], r_z.at[20 + k], zdev[k]))

    for cp in cz:
        cp.wait_recv()
    cc = [to_sibling(code, x, 11)]
    cx = gather_x(code, 22)

    l_gain.wait()
    lane_id = lax.broadcasted_iota(jnp.int32, (128, 128), 1)
    ssq[...] = jnp.zeros_like(ssq)

    def scaled(k, dec, col, squares):
        cols = pl.ds(pl.multiple_of(col, 256), 256)
        normed[k, :, cols] = (dec * gain_v[:, cols]).astype(BF16)
        sq = dec * dec
        return squares + sq[:, :128] + sq[:, 128:]

    def add_squares(k, squares):
        total = jnp.sum(squares, axis=1, keepdims=True)
        ssq[...] += jnp.where(lane_id == k, total, 0.0).reshape(4, 32, 128)

    def near_half(k):
        slot = xs[(4 - k) % 4]
        cc[k].wait_recv()
        squares = jnp.zeros((128, 128), F32)
        for i in range(4):
            j = (2 * c + i) % 4
            dec = jnp.dot(code[slot], w_all[j], preferred_element_type=F32).astype(BF16)
            if k == 0 and i < 2:
                dec_s[:, pl.ds(i * 256, 256)] = dec
            if k == 0 and i == 1:
                dz.append(send(dec_s, dfar.at[x, :, own_half], s_z.at[0], r_z.at[0], zdev[4]))
            squares = scaled(k, dec.astype(F32), zh * 1024 + j * 256, squares)
        add_squares(k, squares)

    dz = []
    near_half(0)
    for cp in pr:
        cp.wait_recv()
    cg = pb[slab, :]
    for k in range(7):
        cg += pb_r[k].astype(F32)
    cg = cg.astype(BF16)
    cg_sh[...] = jnp.where(y == 0, jnp.zeros_like(cg), cg)
    rz = [
        send(cg_sh, ret.at[x, slab, own_half], s_z.at[28 + k], r_z.at[28 + k], downdev[k])
        for k in range(8)
    ]
    sz = [
        send(st_sh, st.at[x, slab, own_half], s_z.at[10 + k], r_z.at[10 + k], zdev[k])
        for k in range(1, 8)
    ]
    for k in range(1, 4):
        cx[k - 1].wait_recv()
        cc.append(to_sibling(code, xs[4 - k], 11 + k))
    for k in range(1, 4):
        near_half(k)
    dz[0].wait_recv()
    dc = [to_sibling(dfar, x, 23)]
    dx = gather_x(dfar, 32)

    for cp in l_gu:
        cp.wait()
    own_m = pl.ds(pl.multiple_of(dp * 32, 32), 32)

    is_end = ((dp + 1) // 2 + 1) % 2
    near = 1 + dp % 2
    other_dp = (dp * 3 + 2) % 5
    opp = 3 * (1 - dp // 2)
    third_dp = is_end * near + (1 - is_end) * opp
    third_slot = 1 + 2 * is_end
    far_m = pl.ds(pl.multiple_of(opp * 32, 32), 32)

    def at_dp(v):
        return (v, y, t)

    def r_in(k, h, slot):
        return r_gu.at[(k * 2 + h) * 4 + slot]

    def third(k, h):
        return pltpu.make_async_remote_copy(
            src_ref=gu_s.at[k, h, opp],
            dst_ref=gu_r.at[k, h, third_slot],
            send_sem=s_gu.at[(k * 2 + h) * 3 + 2],
            recv_sem=r_in(k, h, third_slot),
            device_id=at_dp(third_dp),
            device_id_type=MESH,
        )

    def wait_in(k, h, slot):
        ref = gu_r.at[k, h, slot]
        pltpu.make_async_remote_copy(
            src_ref=ref,
            dst_ref=ref,
            send_sem=s_gu.at[0],
            recv_sem=r_in(k, h, slot),
            device_id=dpdev[1],
            device_id_type=MESH,
        ).wait_recv()

    def group(k):
        slot = xs[(4 - k) % 4]
        dc[k].wait_recv()
        squares = jnp.zeros((128, 128), F32)
        for j in range(4):
            dec = dfar[slot, :, pl.ds(j * 256, 256)].astype(F32)
            squares = scaled(k, dec, (1 - zh) * 1024 + j * 256, squares)
        add_squares(k, squares)

        for h in range(2):
            v = jnp.dot(normed[k], wgu[h], preferred_element_type=F32)
            acc[...] = v
            gu_s[k, h] = v.astype(BF16).reshape(4, 32, 896)
            i = (k * 2 + h) * 3

            @pl.when(is_end == 1)
            def _():
                third(k, h).start()

            send(gu_s.at[k, h, near], gu_r.at[k, h, is_end], s_gu.at[i], r_in(k, h, is_end), at_dp(near))
            send(
                gu_s.at[k, h, other_dp],
                gu_r.at[k, h, 2 * is_end],
                s_gu.at[i + 1],
                r_in(k, h, 2 * is_end),
                at_dp(other_dp),
            )
            gu_own[k, h] = acc[own_m, :]
            gu_far[k, h] = acc[far_m, :]

    def merge(k):
        @pl.when(is_end == 0)
        def _():
            for h in range(2):
                wait_in(k, h, 3)
                gu_s[k, h, opp] = (gu_far[k, h] + gu_r[k, h, 3].astype(F32)).astype(BF16)
                third(k, h).start()

    group(0)
    for k in range(1, 4):
        dx[k - 1].wait_recv()
        dc.append(to_sibling(dfar, xs[4 - k], 23 + k))
    group(1)
    merge(0)
    for cp in rz:
        cp.wait_recv()
    rc = [to_sibling(ret, x, 19)]
    rx = gather_x(ret, 28)
    for cp in sz:
        cp.wait_recv()
    sc = [to_sibling(st, x, 15)]
    sx = gather_x(st, 25)
    group(2)
    merge(1)
    group(3)
    ssq_row[...] = ssq[...].reshape(128, 128).T[:8]
    sq_in = [
        send(ssq_row, ssq_r.at[q - 1], s_gu.at[23 + q], r_gu.at[31 + q], dpdev[q])
        for q in range(1, 4)
    ]
    merge(2)
    merge(3)

    for k in range(1, 4):
        sx[k - 1].wait_recv()
        sc.append(to_sibling(st, xs[4 - k], 15 + k))
    l_grad.wait()
    for cp in sc:
        cp.wait_recv()
    grads = grad_v[...].reshape(4, 2, 4, 16, 128)
    perm = jnp.concatenate([grads[:, :, v].reshape(128, 128) for v in range(4)], axis=0)
    for h in range(4):
        cols = pl.ds(h * 256, 256)
        lhs = st[:, :, cols].reshape(512, 256)
        decg_o[0, cols, :] = lax.dot_general(lhs, perm, FIRST, preferred_element_type=F32)

    for k in range(1, 4):
        rx[k - 1].wait_recv()
        rc.append(to_sibling(ret, xs[4 - k], 19 + k))
    for cp in rc:
        cp.wait_recv()
    l_stin.wait()
    for cp in si:
        cp.wait_recv()
    for v in range(4):
        own_ret = ret[v, own_m, :]
        ing_o[0, pl.ds(v * 32, 32), :] = lax.dot_general(
            own_ret, enc_v[...], LAST, preferred_element_type=F32
        ).astype(BF16)
    rhs = ret[:, :, pl.ds(pl.multiple_of(dp * 256, 256), 256)].reshape(512, 256)
    for h in range(2):
        cols = pl.ds(h * 256, 256)
        lhs = jnp.concatenate(
            [stin_v[:, pl.ds(v * 32, 32), cols].reshape(128, 256) for v in range(4)], axis=0
        )
        encg_o[0, cols, :] = lax.dot_general(lhs, rhs, FIRST, preferred_element_type=F32)

    for cp in sq_in:
        cp.wait_recv()
    total = ssq_row[...] + ssq_r[0] + ssq_r[1] + ssq_r[2]
    total = jnp.concatenate([total, jnp.zeros((120, 128), F32)], axis=0)
    ssq[...] = total.T.reshape(4, 32, 128)
    inv_all = lax.rsqrt(ssq[dp] / D + epsilon)
    for k in range(4):
        for h in range(2):
            wait_in(k, h, 0)
            wait_in(k, h, 1)

        @pl.when(is_end == 0)
        def _():
            for h in range(2):
                wait_in(k, h, 2)
                gu_own[k, h] += gu_r[k, h, 2].astype(F32)

        inv = inv_all[:, k : k + 1]
        rows = pl.ds(pl.multiple_of(xs[(4 - k) % 4] * 32, 32), 32)
        gate, up = [
            (gu_own[k, h] + gu_r[k, h, 0].astype(F32) + gu_r[k, h, 1].astype(F32)) * inv
            for h in range(2)
        ]
        act_o[0, rows, :] = (gate / (1.0 + jnp.exp(-gate)) * up).astype(BF16)

    for cp in pending:
        cp.wait_send()
    for k in range(4):
        for h in range(2):
            third(k, h).wait_send()


def hand_over(a, b, c, d, a_o, b_o, c_o, d_o, a_v, b_v, c_v, d_v, sem):
    steps = ((c, c_v, c_o), (d, d_v, d_o), (a, a_v, a_o), (b, b_v, b_o))
    loads = [pltpu.make_async_copy(src, via, sem.at[i]) for i, (src, via, _) in enumerate(steps)]
    stores = [
        pltpu.make_async_copy(via, dst, sem.at[4 + i]) for i, (_, via, dst) in enumerate(steps)
    ]
    for cp in loads:
        cp.start()
    for load, store in zip(loads, stores):
        load.wait()
        store.start()
    for cp in stores:
        cp.wait()


def per_device(
    outgoing,
    stashed_inputs,
    encoder,
    decoder,
    norm_gain,
    gate_matrix,
    up_matrix,
    grad_decoded,
    stashed_codes,
):
    grad = grad_decoded.reshape(4, 128, 128)
    anywhere = pl.BlockSpec(memory_space=pl.ANY)
    vmem = pl.BlockSpec(memory_space=pltpu.VMEM)
    V = pltpu.VMEM
    DMA = pltpu.SemaphoreType.DMA
    shapes = (
        jax.ShapeDtypeStruct((1, 128, 896), BF16),
        jax.ShapeDtypeStruct((1, 128, 512), BF16),
        jax.ShapeDtypeStruct((1, 512, 256), F32),
        jax.ShapeDtypeStruct((1, 1024, 128), F32),
    )
    results = pl.pallas_call(
        kernel,
        name="section",
        out_shape=shapes,
        in_specs=[anywhere] * 8 + [vmem],
        out_specs=(vmem,) * 4,
        scratch_shapes=[
            V((128, 512), BF16),
            V((512, 1024), BF16),
            V((1, 2048), F32),
            V((4, 128, 128), BF16),
            V((4, 128, 512), BF16),
            V((2, 2048, 896), BF16),
            V((4, 1024, 256), BF16),
            V((128, 512), F32),
            V((128, 512), F32),
            V((128, 512), F32),
            V((3, 32, 512), F32),
            V((32, 512), F32),
            V((16, 512), F32),
            V((16, 512), BF16),
            V((4, 128, 1024), BF16),
            V((16, 512), BF16),
            V((16, 512), BF16),
            V((16, 512), BF16),
            V((4, 128, 1024), BF16),
            V((2, 4, 32, 512), BF16),
            V((128, 512), F32),
            V((8, 16, 512), BF16),
            V((7, 16, 512), BF16),
            V((16, 512), BF16),
            V((4, 128, 1024), BF16),
            V((128, 512), BF16),
            V((4, 128, 1024), BF16),
            V((4, 128, 2048), BF16),
            V((128, 896), F32),
            V((4, 2, 4, 32, 896), BF16),
            V((4, 2, 4, 32, 896), BF16),
            V((4, 2, 32, 896), F32),
            V((4, 2, 32, 896), F32),
            V((4, 32, 128), F32),
            V((8, 128), F32),
            V((3, 8, 128), F32),
            DMA((7,)),
            DMA((2,)),
            DMA((27,)),
            DMA((27,)),
            DMA((36,)),
            DMA((36,)),
            DMA((36,)),
            DMA((36,)),
            DMA((27,)),
            DMA((35,)),
        ],
        compiler_params=pltpu.CompilerParams(
            collective_id=0, has_side_effects=True, vmem_limit_bytes=60 * 2**20
        ),
    )(
        outgoing,
        stashed_inputs,
        encoder,
        decoder,
        norm_gain,
        gate_matrix,
        up_matrix,
        grad,
        stashed_codes,
    )
    return pl.pallas_call(
        hand_over,
        name="hand_over",
        out_shape=shapes,
        in_specs=[anywhere] * 4,
        out_specs=(anywhere,) * 4,
        scratch_shapes=[V(s.shape, s.dtype) for s in shapes] + [DMA((8,))],
        compiler_params=pltpu.CompilerParams(vmem_limit_bytes=60 * 2**20),
    )(*results)


def solution(mesh):
    placed = (
        P("pipe", "dp", "tensor"),
        P("pipe", "dp", "tensor"),
        P("pipe", "tensor", None),
        P("pipe", None, ("dp", "tensor")),
        P("pipe", "dp"),
        P("pipe", "dp", "tensor"),
        P("pipe", "dp", "tensor"),
        P("pipe", None, ("dp", "tensor")),
        P("pipe", ("dp", "tensor"), None),
    )
    return jax.shard_map(
        per_device,
        mesh=mesh,
        in_specs=placed,
        out_specs=(
            P("pipe", "dp", "tensor"),
            P("pipe", "dp", "tensor"),
            P("pipe", "tensor", "dp"),
            P("pipe", None, ("dp", "tensor")),
        ),
        check_vma=False,
    )
```
